128 devices in a mesh: blk: 8 (over y_lo, x), head: 16 (over y_hi, z, core).
Axes of the slice: x: 4, y: 4 (y_hi: 2, y_lo: 2; y = y_hi * 2 + y_lo), z: 4, core: 2. Of those that a mesh axis runs over, the one named last changes fastest.
Arguments:
- q_vals: bfloat16 [8192, 6144], P(('blk', 'head')), may hold values from -96 to 96
- k_vals: bfloat16 [8192, 6144], P(('blk', 'head')), may hold values from -8 to 8
- v_vals: bfloat16 [8192, 6144], P(('blk', 'head')), may hold values from -6 to 6
- q_scale: bfloat16 [8192, 48], P(('blk', 'head')), may hold values from 0.4 to 2.5
- k_scale: bfloat16 [8192, 48], P(('blk', 'head')), may hold values from 0.4 to 2.5
- v_scale: bfloat16 [8192, 48], P(('blk', 'head')), may hold values from 0.3984375 to 2.5
- out_weight: bfloat16 [6144, 6144], P('head'), may hold values from -0.109375 to 0.109375
Outputs:
- targets: bfloat16 [8192, 6144], P('blk', 'head')
The draws below stay inside these ranges and needn't reach their ends.
All inputs are finite; a program needn't handle non-finite values.
Results may differ from the reference program's by a relative error of at most 0.023.
Values may be sent and summed in bfloat16 or wider, within the bound.
No kernel may reach another device: no remote copies, remote signals or barrier semaphores. Data moves between devices by JAX's collectives and lax.ppermute only.
A program may use at most 128 MiB of HBM per device.

```python
import math
import jax
import jax.numpy as jnp
from jax import lax

HEADS = 48
HD = 128
D = 6144
TOKENS = 8192


def key_base(key):
    return jnp.clip(jax.random.normal(key, (TOKENS, D), jnp.float32), -6.0, 6.0)


def block_scales(key):
    key = jax.random.fold_in(key, 7)
    unit = jax.random.uniform(key, (TOKENS, HEADS), jnp.float32)
    lower = jnp.log(jnp.float32(0.4))
    upper = jnp.log(jnp.float32(2.5))
    return jnp.clip(jnp.exp(lower + unit * (upper - lower)), 0.4, 2.5)


def quant_keys(base, scales):
    rounded = scales.astype(jnp.bfloat16).astype(jnp.float32)
    spread = jnp.repeat(rounded, HD, axis=1)
    return jnp.clip(base / spread, -8.0, 8.0)


def draw_k_vals(key, part):
    base = key_base(key)
    scales = block_scales(key)
    return quant_keys(base, scales).astype(jnp.bfloat16)


def draw_k_scale(key, part):
    scales = block_scales(key)
    return scales.astype(jnp.bfloat16)


def draw_q_scale(key, part):
    key = jax.random.fold_in(key, 3)
    scales = block_scales(key)
    return scales.astype(jnp.bfloat16)


def draw_q_vals(key, part):
    key = jax.random.fold_in(key, 1)
    fresh = jnp.clip(jax.random.normal(key, (TOKENS, D), jnp.float32), -6.0, 6.0)
    return fresh.astype(jnp.bfloat16)


def strengthened(values, rng, source, target, parts, factor):
    owner, partner = [(jnp.arange(values.shape[dim]) // (values.shape[dim] // parts)).reshape([-1 if axis == dim else 1 for axis in range(values.ndim)]) for dim in (source, target)]
    chosen = jax.random.permutation(rng, parts)[partner]
    strong = (owner == chosen) | (owner == (partner + parts // 2) % parts)
    return jnp.where(strong, factor * values, values)


def level_of(rng, dims, shards, low, largest):
    def one(axis_at, shards_of):
        draws = jax.random.uniform(jax.random.fold_in(jax.random.fold_in(rng, 6), axis_at), (shards_of,), jnp.float32, low / len(shards), largest / len(shards))
        return jnp.repeat(jnp.exp(draws), dims[axis_at] // shards_of).reshape((-1,) + (1,) * (len(dims) - axis_at - 1))

    loudness = one(*shards[0])
    for cut in shards[1:]:
        loudness = loudness * one(*cut)
    return loudness


def gaussian(rng, extent, deviation, limit, pieces=(), kind=jnp.bfloat16):
    level = level_of(rng, extent, pieces, -0.22, 0.18) if pieces else 1.0
    values = jax.random.normal(rng, extent, jnp.float32) * deviation * level
    return jnp.minimum(jnp.maximum(values, -limit), limit).astype(kind)


def gaussian_with(rng, dims, scale, reach, shards, heavy, held_as=jnp.bfloat16):
    entries = scale * jax.random.normal(rng, dims, jnp.float32)
    if shards:
        entries = entries * level_of(rng, dims, shards, -0.22, 0.18)
    return jnp.clip(strengthened(entries, jax.random.fold_in(rng, 3), *heavy), -reach, reach).astype(held_as)


def setup_inputs(seed: int = 0) -> dict:
    splits = jax.random.split(jax.random.key(seed), 8)
    q_vals = draw_q_vals(jax.random.fold_in(splits[7], 71), 0)
    k_vals = draw_k_vals(jax.random.fold_in(splits[7], 71), 0)
    v_vals = gaussian(splits[2], (TOKENS, D), 1.0, 6.0, ((0, 128),))
    q_scale = draw_q_scale(jax.random.fold_in(splits[7], 71), 0)
    k_scale = draw_k_scale(jax.random.fold_in(splits[7], 71), 0)
    v_scale = jnp.clip(jnp.exp(math.log(2.5) - 1.8364954 * jax.random.uniform(splits[5], (TOKENS, HEADS), jnp.float32) ** level_of(splits[5], (TOKENS, HEADS), ((0, 128),), -0.2, 0.2)), 0.3984375, 2.5).astype(jnp.bfloat16)
    out_weight = gaussian_with(splits[6], (D, D), D ** -0.5, 0.109375, ((0, 16),), (0, 1, 16, 2.0))
    return dict(q_vals=q_vals, k_vals=k_vals, v_vals=v_vals, q_scale=q_scale, k_scale=k_scale, v_scale=v_scale, out_weight=out_weight)


def dequant(vals, scales):
    rows = vals.shape[0]
    full = vals.astype(jnp.float32).reshape(rows, HEADS, HD) * scales.astype(jnp.float32).reshape(rows, HEADS, 1)
    return full.astype(jnp.bfloat16)


def one_head(inputs):
    query, key, value = inputs
    score = jnp.dot(query, key.T, preferred_element_type=jnp.float32) * (1.0 / (HD ** 0.5))
    peak = jnp.max(score, axis=1, keepdims=True)
    expo = jnp.exp(score - peak)
    total = jnp.sum(expo, axis=1, keepdims=True)
    weight = expo.astype(jnp.bfloat16)
    return (jnp.dot(weight, value, preferred_element_type=jnp.float32) / total).astype(jnp.bfloat16)


def reference(q_vals, k_vals, v_vals, q_scale, k_scale, v_scale, out_weight):
    query = jnp.transpose(dequant(q_vals, q_scale), (1, 0, 2))
    key = jnp.transpose(dequant(k_vals, k_scale), (1, 0, 2))
    value = jnp.transpose(dequant(v_vals, v_scale), (1, 0, 2))
    heads_out = lax.map(one_head, (query, key, value))
    attended = jnp.transpose(heads_out, (1, 0, 2)).reshape(TOKENS, D)
    return jnp.dot(attended, out_weight, preferred_element_type=jnp.float32).astype(jnp.bfloat16)
```

```python
import functools

import jax
import jax.numpy as jnp
from jax import lax
from jax.experimental import pallas as pl
from jax.experimental.pallas import tpu as pltpu
from jax.sharding import Mesh, PartitionSpec as P

AXES = ("ylo", "x", "yhi", "z", "core")
HSIZE = 128
HPG = 3
GROUPS = 16
FACTOR = 1.4426950408889634 / HSIZE**0.5
VMEM_BYTES = 56 * 2**20


def group_of(dest):
    ylo, yhi, z = dest // 8, (dest // 4) % 2, dest % 4
    return yhi * 8 + z * 2 + ylo


def dequant_kernel(q_ref, k_ref, v_ref, qs_ref, ks_ref, vs_ref, o_ref, *, head):
    scales = [r[...].astype(jnp.float32) for r in (qs_ref, ks_ref, vs_ref)]
    scales[0] = scales[0] * FACTOR
    for dest in range(GROUPS):
        col = group_of(dest) * HPG + head
        for part, ref in enumerate((q_ref, k_ref, v_ref)):
            vals = ref[:, col * HSIZE : (col + 1) * HSIZE].astype(jnp.float32)
            o_ref[dest, :, part * HSIZE : (part + 1) * HSIZE] = (
                vals * scales[part][:, col : col + 1]
            ).astype(jnp.bfloat16)


def dequant(head, *args):
    tok = args[0].shape[0]
    return pl.pallas_call(
        functools.partial(dequant_kernel, head=head),
        out_shape=jax.ShapeDtypeStruct((GROUPS, tok, 3 * HSIZE), jnp.bfloat16),
        compiler_params=pltpu.CompilerParams(vmem_limit_bytes=VMEM_BYTES),
        cost_estimate=pl.CostEstimate(flops=10**6, bytes_accessed=4 * 10**6, transcendentals=0),
    )(*args)


def attend_kernel(q_ref, *refs, pieces):
    kv = refs[: len(pieces)]
    o_ref, vaug = refs[len(pieces) :]

    @pl.when(pl.program_id(0) == 0)
    def _():
        vaug[:, HSIZE:] = jnp.ones((vaug.shape[0], HSIZE), jnp.bfloat16)
        low = 0
        for ref, size in zip(kv, pieces):
            vaug[low : low + size, :HSIZE] = ref[:, HSIZE:]
            low += size

    query = q_ref[...]

    def score(j):
        return lax.dot_general(
            query, kv[j][:, :HSIZE], (((1,), (1,)), ((), ())), preferred_element_type=jnp.float32
        )

    peak = accum = None
    now = score(0)
    low = 0
    for j, size in enumerate(pieces):
        later = score(j + 1) if j + 1 < len(pieces) else None
        top = jnp.max(now, axis=1, keepdims=True)
        newpeak = top if peak is None else jnp.maximum(peak, top)
        weight = jnp.exp2((now - newpeak).astype(jnp.bfloat16))
        term = jnp.dot(weight, vaug[low : low + size, :], preferred_element_type=jnp.float32)
        accum = term if accum is None else accum * jnp.exp2(peak - newpeak) + term
        peak, now, low = newpeak, later, low + size
    o_ref[...] = (accum[:, :HSIZE] / accum[:, HSIZE:]).astype(jnp.bfloat16)


def attend(qkv, kv):
    rows = qkv.shape[0]
    block = 512
    pieces = tuple(a.shape[0] for a in kv)
    keys = sum(pieces)
    return pl.pallas_call(
        functools.partial(attend_kernel, pieces=pieces),
        grid=(rows // block,),
        in_specs=[pl.BlockSpec((block, HSIZE), lambda i: (i, 0))]
        + [pl.BlockSpec((n, 2 * HSIZE), lambda i: (0, 0)) for n in pieces],
        out_specs=pl.BlockSpec((block, HSIZE), lambda i: (i, 0)),
        out_shape=jax.ShapeDtypeStruct((rows, HSIZE), jnp.bfloat16),
        scratch_shapes=[pltpu.VMEM((keys, 2 * HSIZE), jnp.bfloat16)],
        compiler_params=pltpu.CompilerParams(vmem_limit_bytes=VMEM_BYTES),
        cost_estimate=pl.CostEstimate(
            flops=8 * rows * keys * HSIZE, bytes_accessed=5 * 10**6, transcendentals=rows * keys
        ),
    )(qkv, *kv)


def ring(n, step):
    return [(i, (i + step) % n) for i in range(n)]


def shift_y(a, step):
    perm = []
    for ylo in range(2):
        for yhi in range(2):
            y = (yhi * 2 + ylo + step) % 4
            perm.append((ylo * 2 + yhi, (y % 2) * 2 + y // 2))
    return lax.ppermute(a, ("ylo", "yhi"), perm)


def swap(a):
    return lax.ppermute(a, "core", [(0, 1), (1, 0)])


def ring_gather(a, axis):
    n = 4
    half = a.shape[0] // 2
    before = lax.ppermute(a, axis, ring(n, 1))
    after = lax.ppermute(a, axis, ring(n, -1))
    far0 = lax.ppermute(before[:half], axis, ring(n, 1))
    far1 = lax.ppermute(after[half:], axis, ring(n, -1))
    return [a, before, after, far0, far1]


def spread_weight(out_weight):
    rows = out_weight.shape[0]
    core, ylo, z = lax.axis_index("core"), lax.axis_index("ylo"), lax.axis_index("z")
    w = out_weight.reshape(rows, 2, 4, 2, rows)
    mine = lax.dynamic_index_in_dim(w, core, 3, keepdims=False)
    other = lax.dynamic_index_in_dim(w, 1 - core, 3, keepdims=False)
    got = swap(other)
    base = jnp.where(ylo == core, mine, got)
    base = jnp.transpose(base, (2, 0, 1, 3)).reshape(4, rows, 2 * rows)
    moved = lax.all_to_all(base, "z", split_axis=0, concat_axis=0, tiled=True)
    order = jnp.stack([z, (z + 3) % 4, (z + 1) % 4, (z + 2) % 4])
    moved = jnp.concatenate(
        [lax.dynamic_index_in_dim(moved, order[i], 0, keepdims=False) for i in range(4)], axis=0
    )
    return moved, swap(moved)


def on_device(q_vals, k_vals, v_vals, q_scale, k_scale, v_scale, out_weight):
    cols = out_weight.shape[0]
    parts = (q_vals, k_vals, v_vals, q_scale, k_scale, v_scale)
    gathered = []
    for head in range(HPG):
        spread = dequant(head, *parts)
        qkv = lax.all_to_all(spread, ("ylo", "yhi", "z"), split_axis=0, concat_axis=0, tiled=True)
        qkv = qkv.reshape(-1, 3 * HSIZE)
        kv = ring_gather(qkv[:, HSIZE:], "x")
        kv = [b for a in kv for b in (a, swap(a))]
        gathered.append((qkv, kv))
    w_own, w_other = spread_weight(out_weight)
    attended = [ring_gather(attend(qkv, kv), "z") for qkv, kv in gathered]
    blocks = []
    for i in range(3):
        blocks += [a[i] for a in attended]
    blocks += [jnp.concatenate([a[3], a[4]], axis=0) for a in attended]
    rows = jnp.concatenate(blocks, axis=1)
    half = rows.shape[0] // 2

    def project(w):
        out = jnp.dot(rows, w, preferred_element_type=jnp.float32).astype(jnp.bfloat16)
        return out.reshape(2, half, 2, cols)

    own, other = project(w_own), project(w_other)
    y = lax.axis_index("yhi") * 2 + lax.axis_index("ylo")

    def block(a, step):
        to = (y + step) % 4
        b = lax.dynamic_index_in_dim(a, to % 2, 0, keepdims=False)
        return lax.dynamic_index_in_dim(b, to // 2, 1, keepdims=False)

    def add(*terms):
        return sum(t.astype(jnp.float32) for t in terms)

    bf = jnp.bfloat16
    from_before = shift_y(block(own, 2), 1)
    from_after = shift_y(block(other, 2), -1)
    up = jnp.stack([add(block(own, 1), from_before).astype(bf), block(other, 1)])
    down = jnp.stack([block(own, 3), add(block(other, 3), from_after).astype(bf)])
    up = shift_y(up, 1)
    down = shift_y(down, -1)
    sum_own = add(block(own, 0), up[0], down[0]).astype(bf)
    sum_other = add(block(other, 0), up[1], down[1]).astype(bf)
    got = swap(sum_other)
    core = lax.axis_index("core")
    first = jnp.where(core == 0, sum_own, got).reshape(8, -1, cols)
    second = jnp.where(core == 0, got, sum_own).reshape(8, -1, cols)
    return jnp.stack([first, second], axis=1).reshape(2 * half, cols)


def solution(mesh):
    fine = Mesh(mesh.devices.reshape(2, 4, 2, 4, 2), AXES)
    return jax.shard_map(
        on_device,
        mesh=fine,
        in_specs=(P(AXES, None),) * 6 + (P(("yhi", "z", "core"), None),),
        out_specs=P(("ylo", "x"), ("yhi", "z", "core")),
        check_vma=False,
    )
```

```python
import functools

import jax
import jax.numpy as jnp
from jax import lax
from jax.experimental import pallas as pl
from jax.experimental.pallas import tpu as pltpu
from jax.sharding import Mesh, PartitionSpec as P

AXES = ("ylo", "x", "yhi", "z", "core")
HSIZE = 128
HPG = 3
GROUPS = 16
BLOCK = 512
STATS = 16
FACTOR = 1.4426950408889634 / HSIZE**0.5
SCALE = 0.5
BF = jnp.bfloat16
F32 = jnp.float32
ANY = pl.BlockSpec(memory_space=pl.ANY)


def params(mib):
    return pltpu.CompilerParams(vmem_limit_bytes=mib * 2**20)


def cost(us):
    return pl.CostEstimate(flops=int(us * SCALE * 1.15e9), bytes_accessed=10**5, transcendentals=0)


def gate(a, *tokens):
    return pl.pallas_call(
        lambda *refs: None,
        in_specs=[ANY] * (1 + len(tokens)),
        out_specs=ANY,
        out_shape=jax.ShapeDtypeStruct(a.shape, a.dtype),
        input_output_aliases={0: 0},
        cost_estimate=cost(0.01),
    )(a, *tokens)


def group_of(dest):
    ylo, yhi, z = dest // 8, (dest // 4) % 2, dest % 4
    return yhi * 8 + z * 2 + ylo


def dequant_kernel(q_ref, k_ref, v_ref, qs_ref, ks_ref, vs_ref, *refs, heads):
    o_ref = refs[-1]
    scales = [r[...].astype(F32).T for r in (qs_ref, ks_ref, vs_ref)]
    scales[0] = scales[0] * FACTOR
    for dest in range(GROUPS):
        for i, head in enumerate(heads):
            col = group_of(dest) * HPG + head
            for part, ref in enumerate((q_ref, k_ref, v_ref)):
                at = i if part == 0 else len(heads) + 2 * i + part - 1
                vals = ref[:, col * HSIZE : (col + 1) * HSIZE].astype(F32)
                o_ref[dest, :, at * HSIZE : (at + 1) * HSIZE] = (
                    vals * scales[part][:, col : col + 1]
                ).astype(BF)


def dequant(heads, args, *tokens):
    tok = args[0].shape[0]
    return pl.pallas_call(
        functools.partial(dequant_kernel, heads=heads),
        in_specs=[pl.BlockSpec(memory_space=pltpu.VMEM)] * len(args) + [ANY] * len(tokens),
        out_shape=jax.ShapeDtypeStruct((GROUPS, tok, 3 * len(heads) * HSIZE), BF),
        compiler_params=params(56),
        cost_estimate=cost(3),
    )(*args, *tokens)


def attend_kernel(at_ref, *refs, pieces, queries, tokens):
    q_refs, refs = refs[:queries], refs[queries:]
    kv, refs = refs[: len(pieces)], refs[len(pieces) + tokens :]
    o_refs, vaug = refs[:-1], refs[-1]
    step = pl.program_id(0)

    @pl.when(step == 0)
    def _():
        vaug[:, HSIZE:] = jnp.ones((vaug.shape[0], HSIZE), BF)
        low = 0
        for ref, size in zip(kv, pieces):
            vaug[low : low + size, :HSIZE] = ref[:, HSIZE:]
            low += size

    query = q_refs[0][...]
    if queries > 1:
        query = jnp.where(step < 2, query, q_refs[1][...])

    def score(j):
        return lax.dot_general(
            query, kv[j][:, :HSIZE], (((1,), (1,)), ((), ())), preferred_element_type=F32
        )

    peak = accum = None
    now = score(0)
    low = 0
    for j, size in enumerate(pieces):
        later = score(j + 1) if j + 1 < len(pieces) else None
        top = jnp.max(now, axis=1, keepdims=True)
        newpeak = top if peak is None else jnp.maximum(peak, top)
        weight = jnp.exp2((now - newpeak).astype(BF))
        term = jnp.dot(weight, vaug[low : low + size, :], preferred_element_type=F32)
        accum = term if accum is None else accum * jnp.exp2(peak - newpeak) + term
        peak, now, low = newpeak, later, low + size
    total = accum[:, HSIZE:]
    out = (accum[:, :HSIZE] / total).astype(BF)
    logsum = peak + jnp.log2(total)
    line = logsum.T[:1, :]
    line = jnp.concatenate(
        [line[:, r * HSIZE : (r + 1) * HSIZE] for r in range(BLOCK // HSIZE)], axis=0
    )
    first = line.astype(BF).astype(F32)
    second = (line - first).astype(BF).astype(F32)
    third = line - first - second
    rows = jnp.concatenate([first, second, third, jnp.zeros_like(line)], axis=0).astype(BF)
    for i, o_ref in enumerate(o_refs):

        @pl.when(step // 2 == i)
        def _():
            o_ref[0, :BLOCK, :] = out
            o_ref[0, BLOCK:, :] = rows


def attend(ylo, queries, kv, tokens=()):
    n = len(queries)
    pieces = tuple(a.shape[0] for a, _ in kv)

    def query(i, col):
        return pl.BlockSpec(
            (BLOCK, HSIZE), lambda g, s: (((g if n == 1 else jnp.clip(g - 2 * i, 0, 1)) + s[0]) % 2, col)
        )

    def piece(a, col):
        return pl.BlockSpec((a.shape[0], 2 * HSIZE), lambda g, s: (0, col))

    def result(i):
        return pl.BlockSpec(
            (1, BLOCK + STATS, HSIZE), lambda g, s: (jnp.clip(g - 2 * i, 0, 1), 0, 0)
        )

    return pl.pallas_call(
        functools.partial(attend_kernel, pieces=pieces, queries=n, tokens=len(tokens)),
        grid_spec=pltpu.PrefetchScalarGridSpec(
            num_scalar_prefetch=1,
            grid=(2 * n,),
            in_specs=[
                *[query(i, col) for i, (_, col) in enumerate(queries)],
                *[piece(*a) for a in kv],
                *[ANY] * len(tokens),
            ],
            out_specs=[result(i) for i in range(n)],
            scratch_shapes=[pltpu.VMEM((sum(pieces), 2 * HSIZE), BF)],
        ),
        out_shape=[jax.ShapeDtypeStruct((2, BLOCK + STATS, HSIZE), BF)] * n,
        compiler_params=params(30),
        cost_estimate=cost(6.5 * n),
    )(ylo, *[a for a, _ in queries], *[a for a, _ in kv], *tokens)


def combine_kernel(a, b, *refs):
    outs = refs[-2:]

    def logsum(ref, half):
        s = ref[half, BLOCK:, :].astype(F32)
        s = s[:4] + s[4:8] + s[8:12]
        return jnp.concatenate(
            [jnp.broadcast_to(s[r : r + 1], (HSIZE, HSIZE)).T for r in range(4)], axis=0
        )

    for half in range(2):
        la, lb = logsum(a, half), logsum(b, half)
        top = jnp.maximum(la, lb)
        wa, wb = jnp.exp2(la - top), jnp.exp2(lb - top)
        out = a[half, :BLOCK, :].astype(F32) * wa + b[half, :BLOCK, :].astype(F32) * wb
        outs[half][...] = (out / (wa + wb)).astype(BF)


def combine(a, b, *tokens):
    vmem = pl.BlockSpec(memory_space=pltpu.VMEM)
    return pl.pallas_call(
        combine_kernel,
        in_specs=[vmem] * 2 + [ANY] * len(tokens),
        out_shape=[jax.ShapeDtypeStruct((BLOCK, HSIZE), BF)] * 2,
        compiler_params=params(12),
        cost_estimate=cost(2),
    )(a, b, *tokens)


def ring(n, step):
    return [(i, (i + step) % n) for i in range(n)]


def opposite_y(a, flip=False):
    perm = []
    for yhi in range(2):
        for core in range(2):
            perm.append((yhi * 2 + core, (1 - yhi) * 2 + (1 - core if flip else core)))
    return lax.ppermute(a, ("yhi", "core"), perm)


def swap(a):
    return lax.ppermute(a, "core", [(0, 1), (1, 0)])


def other_ylo(a):
    return lax.ppermute(a, "ylo", [(0, 1), (1, 0)])


def key_pair(a):
    return lax.ppermute(a, "x", [(0, 1), (1, 0), (2, 3), (3, 2)])


def query_pair(a):
    return lax.ppermute(a, "x", [(0, 3), (3, 0), (1, 2), (2, 1)])


def ring_gather(to_next, to_last, to_far):
    return [
        lax.ppermute(to_next, "z", ring(4, 1)),
        lax.ppermute(to_last, "z", ring(4, -1)),
        lax.ppermute(to_far, "z", ring(4, 2)),
    ]


def pack_kernel(z_ref, w_ref, token_ref, *outs):
    half = w_ref.shape[1] // 2
    width = half // 4
    for off, o_ref in zip((0, 1, 3, 2), outs):
        to = lax.rem(z_ref[0] + off, 4)
        for yhi in range(2):
            low = pl.multiple_of(yhi * half + to * width, width)
            o_ref[:, yhi * width : (yhi + 1) * width] = w_ref[:, pl.ds(low, width)]


def pack_weight(z, out_weight, token):
    rows, width = out_weight.shape
    return pl.pallas_call(
        pack_kernel,
        in_specs=[
            pl.BlockSpec(memory_space=pltpu.SMEM),
            pl.BlockSpec(memory_space=pltpu.VMEM),
            ANY,
        ],
        out_shape=[jax.ShapeDtypeStruct((rows, width // 4), BF)] * 4,
        compiler_params=params(56),
        cost_estimate=cost(4),
    )(z, out_weight, token)


def project_kernel(at_ref, *refs, head, before, last, tokens):
    blocks, w, refs = refs[:4], refs[4:12], refs[12:]
    start, refs = refs[:before], refs[before + tokens :]
    outs, (left, right, sems) = refs[: 4 if last else 1], refs[4 if last else 1 :]
    cols = right.shape[1] // 4
    core, apart, yhi = at_ref[0], at_ref[1], at_ref[2]
    copies = []
    for i in range(8):
        for j in range(4):
            low = (lax.rem(yhi + 1 + j // 2, 2) * 2 + lax.rem(core + j, 2)) * cols
            copies.append(
                pltpu.make_async_copy(
                    w[i].at[pl.ds(head * HSIZE, HSIZE), pl.ds(pl.multiple_of(low, cols), cols)],
                    right.at[pl.ds(i * HSIZE, HSIZE), pl.ds(j * cols, cols)],
                    sems.at[len(copies)],
                )
            )
    for copy in copies:
        copy.start()
    for p in range(2):
        low = pl.multiple_of(lax.rem(apart + p, 2) * HSIZE, HSIZE)
        for r in range(4):
            at = (p * 4 + r) * HSIZE
            left[:, at : at + HSIZE] = blocks[r][:, pl.ds(low, HSIZE)]
    for copy in copies:
        copy.wait()
    out = jnp.dot(left[...], right[...], preferred_element_type=F32)
    if before:
        out = out + start[0][...]
    if last:
        for j in range(4):
            outs[j][...] = out[:, j * cols : (j + 1) * cols].astype(BF)
    else:
        outs[0][...] = out


def project(at, head, blocks, weights, before=(), last=False, tokens=()):
    cols = weights[0].shape[0]
    vmem = pl.BlockSpec(memory_space=pltpu.VMEM)
    if last:
        out_shape = [jax.ShapeDtypeStruct((BLOCK, cols), BF)] * 4
    else:
        out_shape = jax.ShapeDtypeStruct((BLOCK, 4 * cols), F32)
    return pl.pallas_call(
        functools.partial(
            project_kernel, head=head, before=len(before), last=last, tokens=len(tokens)
        ),
        in_specs=[pl.BlockSpec(memory_space=pltpu.SMEM)]
        + [vmem] * 4
        + [ANY] * 8
        + [vmem] * len(before)
        + [ANY] * len(tokens),
        out_shape=out_shape,
        scratch_shapes=[
            pltpu.VMEM((BLOCK, 8 * HSIZE), BF),
            pltpu.VMEM((8 * HSIZE, 4 * cols), BF),
            pltpu.SemaphoreType.DMA((32,)),
        ],
        compiler_params=params(20),
        cost_estimate=cost(3),
    )(at, *blocks, *weights, *before, *tokens)


def on_device(q_vals, k_vals, v_vals, q_scale, k_scale, v_scale, out_weight):
    cols = out_weight.shape[0]
    tok = q_vals.shape[0]
    ylo, yhi, z, core = (lax.axis_index(n) for n in ("ylo", "yhi", "z", "core"))
    mine = ylo.reshape(1)
    every = ("ylo", "yhi", "z")

    def exchange(a):
        a = lax.all_to_all(a, every, split_axis=0, concat_axis=0, tiled=True)
        return a.reshape(-1, a.shape[2])

    parts = (q_vals, k_vals, v_vals, q_scale.T, k_scale.T, v_scale.T)
    d1 = dequant((0, 1), parts)
    d2 = dequant((2,), parts, d1)
    packed = pack_weight(z.reshape(1), out_weight, d1)
    e1 = gate(exchange(d1), d2, packed[0])
    q1, kv0, kv1 = (e1[:, i * 2 * HSIZE : (i + 1) * 2 * HSIZE] for i in range(3))
    near0 = key_pair(kv0)
    theirs1 = query_pair(q1)
    s1 = swap(e1)
    e2 = exchange(gate(d2, e1))
    near1 = key_pair(gate(kv1, near0))
    snear0 = swap(near0)
    q2, kv2 = e2[:, :HSIZE], e2[:, HSIZE:]
    theirs2 = query_pair(q2)
    near2 = key_pair(gate(kv2, near1))
    s2 = swap(kv2)
    snear1, snear2 = swap(near1), swap(near2)
    along = ring_gather(*[gate(a, e1) for a in packed[1:]])
    w_own = [packed[0], *along]

    keys0 = [(e1, 1), (s1, 1), (near0, 0), (snear0, 0)]
    keys1 = [(e1, 2), (s1, 2), (near1, 0), (snear1, 0)]
    keys2 = [(kv2, 0), (s2, 0), (near2, 0), (snear2, 0)]

    def widen(keep, send):
        return jnp.concatenate([keep, other_ylo(send)], axis=1)

    def gather(both):
        return [both, *ring_gather(both, both, both)]

    (sent0,) = attend(mine, [(theirs1, 0)], keys0)
    back0 = query_pair(sent0)
    (kept0,) = attend(mine, [(e1, 0)], keys0, (sent0,))
    (sent1,) = attend(mine, [(theirs1, 1)], keys1, (kept0,))
    back1 = query_pair(sent1)
    rows0 = combine(kept0, back0, sent1)
    (kept1,) = attend(mine, [(e1, 1)], keys1, (rows0[0],))
    both0 = widen(*rows0)
    (sent2,) = attend(mine, [(theirs2, 0)], keys2, (kept1, both0))
    set0 = gather(both0)
    back2 = query_pair(sent2)
    rows1 = combine(kept1, back1, sent2)
    (kept2,) = attend(mine, [(q2, 0)], keys2, (rows1[0],))
    set1 = gather(widen(*rows1))
    rows2 = combine(kept2, back2, *set0[1:], *along)
    weights = w_own + [swap(a) for a in w_own]
    set2 = gather(widen(*rows2))
    at = jnp.stack([core, jnp.where(core == ylo, 0, 1), yhi])
    out = project(at, 0, set0, weights, tokens=(rows2[0],))
    out = project(at, 1, set1, weights, (out,))
    out = project(at, 2, set2, weights, (out,), last=True)
    own = out[2].astype(F32) + opposite_y(out[0]).astype(F32)
    other = swap(out[3]).astype(F32) + opposite_y(out[1], flip=True).astype(F32)
    own, other = own.astype(BF), other.astype(BF)
    one = jnp.where(core == 0, own, other).reshape(-1, tok, cols)
    two = jnp.where(core == 0, other, own).reshape(-1, tok, cols)
    return jnp.stack([one, two], axis=1).reshape(-1, cols)


def solution(mesh):
    fine = Mesh(mesh.devices.reshape(2, 4, 2, 4, 2), AXES)
    return jax.shard_map(
        on_device,
        mesh=fine,
        in_specs=(P(AXES, None),) * 6 + (P(("yhi", "z", "core"), None),),
        out_specs=P(("ylo", "x"), ("yhi", "z", "core")),
        check_vma=False,
    )
```

```python
import functools

import jax
import jax.numpy as jnp
from jax import lax
from jax.experimental import pallas as pl
from jax.experimental.pallas import tpu as pltpu
from jax.sharding import Mesh, PartitionSpec as P

AXES = ("ylo", "x", "yhi", "z", "core")
HSIZE = 128
HPG = 3
GROUPS = 16
BLOCK = 512
STATS = 16
FACTOR = 1.4426950408889634 / HSIZE**0.5
SCALE = 1.6
BF = jnp.bfloat16
F32 = jnp.float32
ANY = pl.BlockSpec(memory_space=pl.ANY)


def params(mib):
    return pltpu.CompilerParams(vmem_limit_bytes=mib * 2**20)


def cost(us):
    return pl.CostEstimate(flops=int(us * SCALE * 1.15e9), bytes_accessed=10**5, transcendentals=0)


def gate(a, *tokens):
    return pl.pallas_call(
        lambda *refs: None,
        in_specs=[ANY] * (1 + len(tokens)),
        out_specs=ANY,
        out_shape=jax.ShapeDtypeStruct(a.shape, a.dtype),
        input_output_aliases={0: 0},
        cost_estimate=cost(0.01),
    )(a, *tokens)


def group_of(dest):
    ylo, yhi, z = dest // 8, (dest // 4) % 2, dest % 4
    return yhi * 8 + z * 2 + ylo


def dequant_kernel(q_ref, k_ref, v_ref, qs_ref, ks_ref, vs_ref, *refs, heads):
    o_ref = refs[-1]
    scales = [r[...].astype(F32).T for r in (qs_ref, ks_ref, vs_ref)]
    scales[0] = scales[0] * FACTOR
    for dest in range(GROUPS):
        for i, head in enumerate(heads):
            col = group_of(dest) * HPG + head
            for part, ref in enumerate((q_ref, k_ref, v_ref)):
                at = i if part == 0 else len(heads) + 2 * i + part - 1
                vals = ref[:, col * HSIZE : (col + 1) * HSIZE].astype(F32)
                o_ref[dest, :, at * HSIZE : (at + 1) * HSIZE] = (
                    vals * scales[part][:, col : col + 1]
                ).astype(BF)


def dequant(heads, args, *tokens):
    tok = args[0].shape[0]
    return pl.pallas_call(
        functools.partial(dequant_kernel, heads=heads),
        in_specs=[pl.BlockSpec(memory_space=pltpu.VMEM)] * len(args) + [ANY] * len(tokens),
        out_shape=jax.ShapeDtypeStruct((GROUPS, tok, 3 * len(heads) * HSIZE), BF),
        compiler_params=params(56),
        cost_estimate=cost(3),
    )(*args, *tokens)


def attend_kernel(at_ref, *refs, pieces, queries, tokens):
    q_refs, refs = refs[:queries], refs[queries:]
    kv, refs = refs[: len(pieces)], refs[len(pieces) + tokens :]
    o_refs, vaug = refs[:-1], refs[-1]
    step = pl.program_id(0)

    @pl.when(step == 0)
    def _():
        vaug[:, HSIZE:] = jnp.ones((vaug.shape[0], HSIZE), BF)
        low = 0
        for ref, size in zip(kv, pieces):
            vaug[low : low + size, :HSIZE] = ref[:, HSIZE:]
            low += size

    query = q_refs[0][...]
    if queries > 1:
        query = jnp.where(step < 2, query, q_refs[1][...])

    def score(j):
        return lax.dot_general(
            query, kv[j][:, :HSIZE], (((1,), (1,)), ((), ())), preferred_element_type=F32
        )

    peak = accum = None
    now = score(0)
    low = 0
    for j, size in enumerate(pieces):
        later = score(j + 1) if j + 1 < len(pieces) else None
        top = jnp.max(now, axis=1, keepdims=True)
        newpeak = top if peak is None else jnp.maximum(peak, top)
        weight = jnp.exp2((now - newpeak).astype(BF))
        term = jnp.dot(weight, vaug[low : low + size, :], preferred_element_type=F32)
        accum = term if accum is None else accum * jnp.exp2(peak - newpeak) + term
        peak, now, low = newpeak, later, low + size
    total = accum[:, HSIZE:]
    out = (accum[:, :HSIZE] / total).astype(BF)
    logsum = peak + jnp.log2(total)
    line = logsum.T[:1, :]
    line = jnp.concatenate(
        [line[:, r * HSIZE : (r + 1) * HSIZE] for r in range(BLOCK // HSIZE)], axis=0
    )
    first = line.astype(BF).astype(F32)
    second = (line - first).astype(BF).astype(F32)
    third = line - first - second
    rows = jnp.concatenate([first, second, third, jnp.zeros_like(line)], axis=0).astype(BF)
    for i, o_ref in enumerate(o_refs):

        @pl.when(step // 2 == i)
        def _():
            o_ref[0, :BLOCK, :] = out
            o_ref[0, BLOCK:, :] = rows


def attend(ylo, queries, kv, tokens=()):
    n = len(queries)
    pieces = tuple(a.shape[0] for a, _ in kv)

    def query(i, col):
        return pl.BlockSpec(
            (BLOCK, HSIZE), lambda g, s: (((g if n == 1 else jnp.clip(g - 2 * i, 0, 1)) + s[0]) % 2, col)
        )

    def piece(a, col):
        return pl.BlockSpec((a.shape[0], 2 * HSIZE), lambda g, s: (0, col))

    def result(i):
        return pl.BlockSpec(
            (1, BLOCK + STATS, HSIZE), lambda g, s: (jnp.clip(g - 2 * i, 0, 1), 0, 0)
        )

    return pl.pallas_call(
        functools.partial(attend_kernel, pieces=pieces, queries=n, tokens=len(tokens)),
        grid_spec=pltpu.PrefetchScalarGridSpec(
            num_scalar_prefetch=1,
            grid=(2 * n,),
            in_specs=[
                *[query(i, col) for i, (_, col) in enumerate(queries)],
                *[piece(*a) for a in kv],
                *[ANY] * len(tokens),
            ],
            out_specs=[result(i) for i in range(n)],
            scratch_shapes=[pltpu.VMEM((sum(pieces), 2 * HSIZE), BF)],
        ),
        out_shape=[jax.ShapeDtypeStruct((2, BLOCK + STATS, HSIZE), BF)] * n,
        compiler_params=params(30),
        cost_estimate=cost(6.5 * n),
    )(ylo, *[a for a, _ in queries], *[a for a, _ in kv], *tokens)


def combine_kernel(a, b, *refs):
    outs = refs[-2:]

    def logsum(ref, half):
        s = ref[half, BLOCK:, :].astype(F32)
        s = s[:4] + s[4:8] + s[8:12]
        return jnp.concatenate(
            [jnp.broadcast_to(s[r : r + 1], (HSIZE, HSIZE)).T for r in range(4)], axis=0
        )

    for half in range(2):
        la, lb = logsum(a, half), logsum(b, half)
        top = jnp.maximum(la, lb)
        wa, wb = jnp.exp2(la - top), jnp.exp2(lb - top)
        out = a[half, :BLOCK, :].astype(F32) * wa + b[half, :BLOCK, :].astype(F32) * wb
        outs[half][...] = (out / (wa + wb)).astype(BF)


def combine(a, b, *tokens):
    vmem = pl.BlockSpec(memory_space=pltpu.VMEM)
    return pl.pallas_call(
        combine_kernel,
        in_specs=[vmem] * 2 + [ANY] * len(tokens),
        out_shape=[jax.ShapeDtypeStruct((BLOCK, HSIZE), BF)] * 2,
        compiler_params=params(12),
        cost_estimate=cost(2),
    )(a, b, *tokens)


def ring(n, step):
    return [(i, (i + step) % n) for i in range(n)]


def opposite_y(a, flip=False):
    perm = []
    for yhi in range(2):
        for core in range(2):
            perm.append((yhi * 2 + core, (1 - yhi) * 2 + (1 - core if flip else core)))
    return lax.ppermute(a, ("yhi", "core"), perm)


def swap(a):
    return lax.ppermute(a, "core", [(0, 1), (1, 0)])


def other_ylo(a):
    return lax.ppermute(a, "ylo", [(0, 1), (1, 0)])


def key_pair(a):
    return lax.ppermute(a, "x", [(0, 1), (1, 0), (2, 3), (3, 2)])


def query_pair(a):
    return lax.ppermute(a, "x", [(0, 3), (3, 0), (1, 2), (2, 1)])


def ring_gather(to_next, to_last, to_far):
    return [
        lax.ppermute(to_next, "z", ring(4, 1)),
        lax.ppermute(to_last, "z", ring(4, -1)),
        lax.ppermute(to_far, "z", ring(4, 2)),
    ]


def pack_kernel(w_ref, token_ref, o_ref):
    half = w_ref.shape[1] // 2
    width = half // 4
    for to in range(4):
        for yhi in range(2):
            low = yhi * half + to * width
            o_ref[to, :, yhi * width : (yhi + 1) * width] = w_ref[:, low : low + width]


def pack_weight(out_weight, token):
    rows, width = out_weight.shape
    return pl.pallas_call(
        pack_kernel,
        in_specs=[pl.BlockSpec(memory_space=pltpu.VMEM), ANY],
        out_shape=jax.ShapeDtypeStruct((4, rows, width // 4), BF),
        compiler_params=params(56),
        cost_estimate=cost(4),
    )(out_weight, token)


def project_kernel(at_ref, *refs, head, before, last, tokens):
    blocks, w, refs = refs[:4], refs[4:6], refs[6:]
    start, refs = refs[:before], refs[before + tokens :]
    outs, (left, right, sems) = refs[: 4 if last else 1], refs[4 if last else 1 :]
    cols = right.shape[1] // 4
    core, apart, yhi, z = at_ref[0], at_ref[1], at_ref[2], at_ref[3]
    copies = []
    for i, off in enumerate((0, 3, 1, 2) * 2):
        group = w[i // 4].at[lax.rem(z + off, 4)]
        for j in range(4):
            low = (lax.rem(yhi + 1 + j // 2, 2) * 2 + lax.rem(core + j, 2)) * cols
            copies.append(
                pltpu.make_async_copy(
                    group.at[pl.ds(head * HSIZE, HSIZE), pl.ds(pl.multiple_of(low, cols), cols)],
                    right.at[pl.ds(i * HSIZE, HSIZE), pl.ds(j * cols, cols)],
                    sems.at[len(copies)],
                )
            )
    for copy in copies:
        copy.start()
    for p in range(2):
        low = pl.multiple_of(lax.rem(apart + p, 2) * HSIZE, HSIZE)
        for r in range(4):
            at = (p * 4 + r) * HSIZE
            left[:, at : at + HSIZE] = blocks[r][:, pl.ds(low, HSIZE)]
    for copy in copies:
        copy.wait()
    out = jnp.dot(left[...], right[...], preferred_element_type=F32)
    if before:
        out = out + start[0][...]
    if last:
        for j in range(4):
            outs[j][...] = out[:, j * cols : (j + 1) * cols].astype(BF)
    else:
        outs[0][...] = out


def project(at, head, blocks, weights, before=(), last=False, tokens=()):
    cols = weights[0].shape[1]
    vmem = pl.BlockSpec(memory_space=pltpu.VMEM)
    if last:
        out_shape = [jax.ShapeDtypeStruct((BLOCK, cols), BF)] * 4
    else:
        out_shape = jax.ShapeDtypeStruct((BLOCK, 4 * cols), F32)
    return pl.pallas_call(
        functools.partial(
            project_kernel, head=head, before=len(before), last=last, tokens=len(tokens)
        ),
        in_specs=[pl.BlockSpec(memory_space=pltpu.SMEM)]
        + [vmem] * 4
        + [ANY] * 2
        + [vmem] * len(before)
        + [ANY] * len(tokens),
        out_shape=out_shape,
        scratch_shapes=[
            pltpu.VMEM((BLOCK, 8 * HSIZE), BF),
            pltpu.VMEM((8 * HSIZE, 4 * cols), BF),
            pltpu.SemaphoreType.DMA((32,)),
        ],
        compiler_params=params(20),
        cost_estimate=cost(3),
    )(at, *blocks, *weights, *before, *tokens)


def on_device(q_vals, k_vals, v_vals, q_scale, k_scale, v_scale, out_weight):
    cols = out_weight.shape[0]
    tok = q_vals.shape[0]
    ylo, yhi, z, core = (lax.axis_index(n) for n in ("ylo", "yhi", "z", "core"))
    mine = ylo.reshape(1)
    every = ("ylo", "yhi", "z")

    def exchange(a):
        a = lax.all_to_all(a, every, split_axis=0, concat_axis=0, tiled=True)
        return a.reshape(-1, a.shape[2])

    parts = (q_vals, k_vals, v_vals, q_scale.T, k_scale.T, v_scale.T)
    d1 = dequant((0, 1), parts)
    d2 = dequant((2,), parts, d1)
    packed = pack_weight(out_weight, d1)
    e1 = gate(exchange(d1), d2, packed)
    q1, kv0, kv1 = (e1[:, i * 2 * HSIZE : (i + 1) * 2 * HSIZE] for i in range(3))
    near0 = key_pair(kv0)
    theirs1 = query_pair(q1)
    s1 = swap(e1)
    e2 = exchange(gate(d2, e1))
    near1 = key_pair(gate(kv1, near0))
    snear0 = swap(near0)
    q2, kv2 = e2[:, :HSIZE], e2[:, HSIZE:]
    theirs2 = query_pair(q2)
    near2 = key_pair(gate(kv2, near1))
    s2 = swap(kv2)
    snear1, snear2 = swap(near1), swap(near2)
    moved = lax.all_to_all(gate(packed, e2), "z", split_axis=0, concat_axis=0, tiled=True)

    keys0 = [(e1, 1), (s1, 1), (near0, 0), (snear0, 0)]
    keys1 = [(e1, 2), (s1, 2), (near1, 0), (snear1, 0)]
    keys2 = [(kv2, 0), (s2, 0), (near2, 0), (snear2, 0)]

    def widen(keep, send):
        return jnp.concatenate([keep, other_ylo(send)], axis=1)

    def gather(both):
        return [both, *ring_gather(both, both, both)]

    (kept0,) = attend(mine, [(e1, 0)], keys0)
    (sent0,) = attend(mine, [(theirs1, 0)], keys0, (kept0,))
    back0 = query_pair(sent0)
    (sent1,) = attend(mine, [(theirs1, 1)], keys1, (sent0,))
    back1 = query_pair(sent1)
    rows0 = combine(kept0, back0, sent1)
    (kept1,) = attend(mine, [(e1, 1)], keys1, (rows0[0],))
    both0 = widen(*rows0)
    rows1 = combine(kept1, back1)
    (sent2,) = attend(mine, [(theirs2, 0)], keys2, (rows1[0], both0))
    set0 = gather(both0)
    back2 = query_pair(sent2)
    both1 = widen(*rows1)
    (kept2,) = attend(mine, [(q2, 0)], keys2, (sent2, both1))
    set1 = gather(both1)
    rows2 = combine(kept2, back2, *set0[1:])
    moved = gate(moved, rows2[0])
    weights = [moved, swap(moved)]
    both2 = widen(*rows2)
    set2 = gather(both2)
    at = jnp.stack([core, jnp.where(core == ylo, 0, 1), yhi, z])
    out = project(at, 0, set0, weights, tokens=(both2, *set1[1:]))
    out = project(at, 1, set1, weights, (out,))
    out = project(at, 2, set2, weights, (out,), last=True)
    own = out[2].astype(F32) + opposite_y(out[0]).astype(F32)
    other = swap(out[3]).astype(F32) + opposite_y(out[1], flip=True).astype(F32)
    own, other = own.astype(BF), other.astype(BF)
    one = jnp.where(core == 0, own, other).reshape(-1, tok, cols)
    two = jnp.where(core == 0, other, own).reshape(-1, tok, cols)
    return jnp.stack([one, two], axis=1).reshape(-1, cols)


def solution(mesh):
    fine = Mesh(mesh.devices.reshape(2, 4, 2, 4, 2), AXES)
    return jax.shard_map(
        on_device,
        mesh=fine,
        in_specs=(P(AXES, None),) * 6 + (P(("yhi", "z", "core"), None),),
        out_specs=P(("ylo", "x"), ("yhi", "z", "core")),
        check_vma=False,
    )
```

```python
import functools

import jax
import jax.numpy as jnp
from jax import lax
from jax.experimental import pallas as pl
from jax.experimental.pallas import tpu as pltpu
from jax.sharding import Mesh, PartitionSpec as P

AXES = ("ylo", "x", "yhi", "z", "core")
HSIZE = 128
HPG = 3
GROUPS = 16
BLOCK = 512
STATS = 16
FACTOR = 1.4426950408889634 / HSIZE**0.5
SCALE = 1.6
BF = jnp.bfloat16
F32 = jnp.float32
ANY = pl.BlockSpec(memory_space=pl.ANY)


def params(mib):
    return pltpu.CompilerParams(vmem_limit_bytes=mib * 2**20)


def cost(us):
    return pl.CostEstimate(flops=int(us * SCALE * 1.15e9), bytes_accessed=10**5, transcendentals=0)


def gate(a, *tokens):
    return pl.pallas_call(
        lambda *refs: None,
        in_specs=[ANY] * (1 + len(tokens)),
        out_specs=ANY,
        out_shape=jax.ShapeDtypeStruct(a.shape, a.dtype),
        input_output_aliases={0: 0},
        cost_estimate=cost(0.01),
    )(a, *tokens)


def group_of(dest):
    ylo, yhi, z = dest // 8, (dest // 4) % 2, dest % 4
    return yhi * 8 + z * 2 + ylo


def dequant_kernel(q_ref, k_ref, v_ref, qs_ref, ks_ref, vs_ref, *refs, heads):
    o_ref = refs[-1]
    scales = [r[...].astype(F32).T for r in (qs_ref, ks_ref, vs_ref)]
    scales[0] = scales[0] * FACTOR
    for dest in range(GROUPS):
        for i, head in enumerate(heads):
            col = group_of(dest) * HPG + head
            for part, ref in enumerate((q_ref, k_ref, v_ref)):
                at = i if part == 0 else len(heads) + 2 * i + part - 1
                vals = ref[:, col * HSIZE : (col + 1) * HSIZE].astype(F32)
                o_ref[dest, :, at * HSIZE : (at + 1) * HSIZE] = (
                    vals * scales[part][:, col : col + 1]
                ).astype(BF)


def dequant(heads, args, *tokens):
    tok = args[0].shape[0]
    return pl.pallas_call(
        functools.partial(dequant_kernel, heads=heads),
        in_specs=[pl.BlockSpec(memory_space=pltpu.VMEM)] * len(args) + [ANY] * len(tokens),
        out_shape=jax.ShapeDtypeStruct((GROUPS, tok, 3 * len(heads) * HSIZE), BF),
        compiler_params=params(56),
        cost_estimate=cost(3),
    )(*args, *tokens)


def attend_kernel(at_ref, *refs, pieces, queries, tokens):
    q_refs, refs = refs[:queries], refs[queries:]
    kv, refs = refs[: len(pieces)], refs[len(pieces) + tokens :]
    o_refs, vaug = refs[:-1], refs[-1]
    step = pl.program_id(0)

    @pl.when(step == 0)
    def _():
        vaug[:, HSIZE:] = jnp.ones((vaug.shape[0], HSIZE), BF)
        low = 0
        for ref, size in zip(kv, pieces):
            vaug[low : low + size, :HSIZE] = ref[:, HSIZE:]
            low += size

    query = q_refs[0][...]
    if queries > 1:
        query = jnp.where(step < 2, query, q_refs[1][...])

    def score(j):
        return lax.dot_general(
            query, kv[j][:, :HSIZE], (((1,), (1,)), ((), ())), preferred_element_type=F32
        )

    peak = accum = None
    now = score(0)
    low = 0
    for j, size in enumerate(pieces):
        later = score(j + 1) if j + 1 < len(pieces) else None
        top = jnp.max(now, axis=1, keepdims=True)
        newpeak = top if peak is None else jnp.maximum(peak, top)
        weight = jnp.exp2((now - newpeak).astype(BF))
        term = jnp.dot(weight, vaug[low : low + size, :], preferred_element_type=F32)
        accum = term if accum is None else accum * jnp.exp2(peak - newpeak) + term
        peak, now, low = newpeak, later, low + size
    total = accum[:, HSIZE:]
    out = (accum[:, :HSIZE] / total).astype(BF)
    logsum = peak + jnp.log2(total)
    line = logsum.T[:1, :]
    line = jnp.concatenate(
        [line[:, r * HSIZE : (r + 1) * HSIZE] for r in range(BLOCK // HSIZE)], axis=0
    )
    first = line.astype(BF).astype(F32)
    second = (line - first).astype(BF).astype(F32)
    third = line - first - second
    rows = jnp.concatenate([first, second, third, jnp.zeros_like(line)], axis=0).astype(BF)
    for i, o_ref in enumerate(o_refs):

        @pl.when(step // 2 == i)
        def _():
            o_ref[0, :BLOCK, :] = out
            o_ref[0, BLOCK:, :] = rows


def attend(ylo, queries, kv, tokens=()):
    n = len(queries)
    pieces = tuple(a.shape[0] for a, _ in kv)

    def query(i, col):
        return pl.BlockSpec(
            (BLOCK, HSIZE), lambda g, s: (((g if n == 1 else jnp.clip(g - 2 * i, 0, 1)) + s[0]) % 2, col)
        )

    def piece(a, col):
        return pl.BlockSpec((a.shape[0], 2 * HSIZE), lambda g, s: (0, col))

    def result(i):
        return pl.BlockSpec(
            (1, BLOCK + STATS, HSIZE), lambda g, s: (jnp.clip(g - 2 * i, 0, 1), 0, 0)
        )

    return pl.pallas_call(
        functools.partial(attend_kernel, pieces=pieces, queries=n, tokens=len(tokens)),
        grid_spec=pltpu.PrefetchScalarGridSpec(
            num_scalar_prefetch=1,
            grid=(2 * n,),
            in_specs=[
                *[query(i, col) for i, (_, col) in enumerate(queries)],
                *[piece(*a) for a in kv],
                *[ANY] * len(tokens),
            ],
            out_specs=[result(i) for i in range(n)],
            scratch_shapes=[pltpu.VMEM((sum(pieces), 2 * HSIZE), BF)],
        ),
        out_shape=[jax.ShapeDtypeStruct((2, BLOCK + STATS, HSIZE), BF)] * n,
        compiler_params=params(30),
        cost_estimate=cost(6.5 * n),
    )(ylo, *[a for a, _ in queries], *[a for a, _ in kv], *tokens)


def combine_kernel(a, b, *refs):
    outs = refs[-2:]

    def logsum(ref, half):
        s = ref[half, BLOCK:, :].astype(F32)
        s = s[:4] + s[4:8] + s[8:12]
        return jnp.concatenate(
            [jnp.broadcast_to(s[r : r + 1], (HSIZE, HSIZE)).T for r in range(4)], axis=0
        )

    for half in range(2):
        la, lb = logsum(a, half), logsum(b, half)
        top = jnp.maximum(la, lb)
        wa, wb = jnp.exp2(la - top), jnp.exp2(lb - top)
        out = a[half, :BLOCK, :].astype(F32) * wa + b[half, :BLOCK, :].astype(F32) * wb
        outs[half][...] = (out / (wa + wb)).astype(BF)


def combine(a, b, *tokens):
    vmem = pl.BlockSpec(memory_space=pltpu.VMEM)
    return pl.pallas_call(
        combine_kernel,
        in_specs=[vmem] * 2 + [ANY] * len(tokens),
        out_shape=[jax.ShapeDtypeStruct((BLOCK, HSIZE), BF)] * 2,
        compiler_params=params(12),
        cost_estimate=cost(2),
    )(a, b, *tokens)


def ring(n, step):
    return [(i, (i + step) % n) for i in range(n)]


def opposite_y(a, flip=False):
    perm = []
    for yhi in range(2):
        for core in range(2):
            perm.append((yhi * 2 + core, (1 - yhi) * 2 + (1 - core if flip else core)))
    return lax.ppermute(a, ("yhi", "core"), perm)


def swap(a):
    return lax.ppermute(a, "core", [(0, 1), (1, 0)])


def other_ylo(a):
    return lax.ppermute(a, "ylo", [(0, 1), (1, 0)])


def key_pair(a):
    return lax.ppermute(a, "x", [(0, 1), (1, 0), (2, 3), (3, 2)])


def query_pair(a):
    return lax.ppermute(a, "x", [(0, 3), (3, 0), (1, 2), (2, 1)])


def ring_gather(to_next, to_last, to_far):
    return [
        lax.ppermute(to_next, "z", ring(4, 1)),
        lax.ppermute(to_last, "z", ring(4, -1)),
        lax.ppermute(to_far, "z", ring(4, 2)),
    ]


def pack_kernel(w_ref, token_ref, o_ref):
    half = w_ref.shape[1] // 2
    width = half // 4
    for to in range(4):
        for yhi in range(2):
            low = yhi * half + to * width
            o_ref[to, :, yhi * width : (yhi + 1) * width] = w_ref[:, low : low + width]


def pack_weight(out_weight, token):
    rows, width = out_weight.shape
    return pl.pallas_call(
        pack_kernel,
        in_specs=[pl.BlockSpec(memory_space=pltpu.VMEM), ANY],
        out_shape=jax.ShapeDtypeStruct((4, rows, width // 4), BF),
        compiler_params=params(56),
        cost_estimate=cost(4),
    )(out_weight, token)


def project_kernel(at_ref, *refs, head, before, last, near, tokens):
    blocks, w, refs = refs[:4], refs[4:6], refs[6:]
    start, refs = refs[:before], refs[before + tokens :]
    outs, (left, right, sems) = refs[:2], refs[2:]
    sides = (near,) if last else (0, 1)
    cols = right.shape[2] // 2
    core, apart, yhi, z = at_ref[0], at_ref[1], at_ref[2], at_ref[3]
    copies = []
    for n, side in enumerate(sides):
        for i, off in enumerate((0, 3, 1, 2) * 2):
            group = w[i // 4].at[lax.rem(z + off, 4)]
            for j in range(2):
                low = (lax.rem(yhi + 1 + side, 2) * 2 + lax.rem(core + j, 2)) * cols
                copies.append(
                    pltpu.make_async_copy(
                        group.at[pl.ds(head * HSIZE, HSIZE), pl.ds(pl.multiple_of(low, cols), cols)],
                        right.at[n, pl.ds(i * HSIZE, HSIZE), pl.ds(j * cols, cols)],
                        sems.at[len(copies)],
                    )
                )
    for copy in copies:
        copy.start()
    for p in range(2):
        low = pl.multiple_of(lax.rem(apart + p, 2) * HSIZE, HSIZE)
        for r in range(4):
            at = (p * 4 + r) * HSIZE
            left[:, at : at + HSIZE] = blocks[r][:, pl.ds(low, HSIZE)]
    for n in range(len(sides)):
        for copy in copies[16 * n : 16 * n + 16]:
            copy.wait()
        out = jnp.dot(left[...], right[n], preferred_element_type=F32)
        if before:
            out = out + start[n][...]
        if last:
            for j in range(2):
                outs[j][...] = out[:, j * cols : (j + 1) * cols].astype(BF)
        else:
            outs[n][...] = out


def project(at, head, blocks, weights, before=(), last=False, near=0, tokens=()):
    cols = weights[0].shape[1]
    vmem = pl.BlockSpec(memory_space=pltpu.VMEM)
    sides = 1 if last else 2
    if last:
        out_shape = [jax.ShapeDtypeStruct((BLOCK, cols), BF)] * 2
    else:
        out_shape = [jax.ShapeDtypeStruct((BLOCK, 2 * cols), F32)] * 2
    return pl.pallas_call(
        functools.partial(
            project_kernel, head=head, before=len(before), last=last, near=near, tokens=len(tokens)
        ),
        in_specs=[pl.BlockSpec(memory_space=pltpu.SMEM)]
        + [vmem] * 4
        + [ANY] * 2
        + [vmem] * len(before)
        + [ANY] * len(tokens),
        out_shape=out_shape,
        scratch_shapes=[
            pltpu.VMEM((BLOCK, 8 * HSIZE), BF),
            pltpu.VMEM((sides, 8 * HSIZE, 2 * cols), BF),
            pltpu.SemaphoreType.DMA((16 * sides,)),
        ],
        compiler_params=params(20),
        cost_estimate=cost(0.05 if near else 1.5 * sides),
    )(at, *blocks, *weights, *before, *tokens)


def finish_kernel(core_ref, a, b, c, d, o_ref):
    own = (a[...].astype(F32) + b[...].astype(F32)).astype(BF)
    other = (c[...].astype(F32) + d[...].astype(F32)).astype(BF)
    tok = o_ref.shape[2]
    for i in range(o_ref.shape[0]):
        rows = slice(i * tok, (i + 1) * tok)
        o_ref[i, core_ref[0]] = own[rows]
        o_ref[i, 1 - core_ref[0]] = other[rows]


def finish(core, tok, *terms):
    rows, cols = terms[0].shape
    vmem = pl.BlockSpec(memory_space=pltpu.VMEM)
    return pl.pallas_call(
        finish_kernel,
        in_specs=[pl.BlockSpec(memory_space=pltpu.SMEM)] + [vmem] * 4,
        out_shape=jax.ShapeDtypeStruct((rows // tok, 2, tok, cols), BF),
        compiler_params=params(12),
        cost_estimate=cost(1),
    )(core, *terms).reshape(2 * rows, cols)


def on_device(q_vals, k_vals, v_vals, q_scale, k_scale, v_scale, out_weight):
    tok = q_vals.shape[0]
    ylo, yhi, z, core = (lax.axis_index(n) for n in ("ylo", "yhi", "z", "core"))
    mine = ylo.reshape(1)
    every = ("ylo", "yhi", "z")

    def exchange(a):
        a = lax.all_to_all(a, every, split_axis=0, concat_axis=0, tiled=True)
        return a.reshape(-1, a.shape[2])

    parts = (q_vals, k_vals, v_vals, q_scale.T, k_scale.T, v_scale.T)
    d1 = dequant((0, 1), parts)
    d2 = dequant((2,), parts, d1)
    packed = pack_weight(out_weight, d1)
    e1 = gate(exchange(d1), d2, packed)
    q1, kv0, kv1 = (e1[:, i * 2 * HSIZE : (i + 1) * 2 * HSIZE] for i in range(3))
    near0 = key_pair(kv0)
    theirs1 = query_pair(q1)
    s1 = swap(e1)
    e2 = exchange(gate(d2, e1))
    near1 = key_pair(gate(kv1, near0))
    snear0 = swap(near0)
    q2, kv2 = e2[:, :HSIZE], e2[:, HSIZE:]
    theirs2 = query_pair(q2)
    near2 = key_pair(gate(kv2, near1))
    s2 = swap(kv2)
    snear1, snear2 = swap(near1), swap(near2)
    moved = lax.all_to_all(gate(packed, e2), "z", split_axis=0, concat_axis=0, tiled=True)

    keys0 = [(e1, 1), (s1, 1), (near0, 0), (snear0, 0)]
    keys1 = [(e1, 2), (s1, 2), (near1, 0), (snear1, 0)]
    keys2 = [(kv2, 0), (s2, 0), (near2, 0), (snear2, 0)]

    def widen(keep, send):
        return jnp.concatenate([keep, other_ylo(send)], axis=1)

    def gather(both):
        return [both, *ring_gather(both, both, both)]

    (kept0,) = attend(mine, [(e1, 0)], keys0)
    (sent0,) = attend(mine, [(theirs1, 0)], keys0, (kept0,))
    back0 = query_pair(sent0)
    (sent1,) = attend(mine, [(theirs1, 1)], keys1, (sent0,))
    back1 = query_pair(sent1)
    rows0 = combine(kept0, back0, sent1)
    (kept1,) = attend(mine, [(e1, 1)], keys1, (rows0[0],))
    both0 = widen(*rows0)
    rows1 = combine(kept1, back1, both0)
    (sent2,) = attend(mine, [(theirs2, 0)], keys2, (rows1[0],))
    set0 = gather(both0)
    back2 = query_pair(sent2)
    both1 = widen(*rows1)
    (kept2,) = attend(mine, [(q2, 0)], keys2, (sent2,))
    set1 = gather(both1)
    rows2 = combine(kept2, back2, *set0[1:], both1)
    moved = gate(moved, rows2[0])
    weights = [moved, swap(moved)]
    both2 = widen(*rows2)
    set2 = gather(both2)
    at = jnp.stack([core, jnp.where(core == ylo, 0, 1), yhi, z])
    out = project(at, 0, set0, weights, tokens=(both2, *set1[1:3]))
    out = project(at, 1, set1, weights, out)
    far = project(at, 2, set2, weights, out[:1], last=True)
    here = project(at, 2, set2, weights, out[1:], last=True, near=1, tokens=far[:1])
    return finish(
        core.reshape(1),
        tok,
        here[0],
        opposite_y(far[0]),
        swap(here[1]),
        opposite_y(far[1], flip=True),
    )


def solution(mesh):
    fine = Mesh(mesh.devices.reshape(2, 4, 2, 4, 2), AXES)
    return jax.shard_map(
        on_device,
        mesh=fine,
        in_specs=(P(AXES, None),) * 6 + (P(("yhi", "z", "core"), None),),
        out_specs=P(("ylo", "x"), ("yhi", "z", "core")),
        check_vma=False,
    )
```

```python
import functools

import jax
import jax.numpy as jnp
from jax import lax
from jax.experimental import pallas as pl
from jax.experimental.pallas import tpu as pltpu
from jax.sharding import Mesh, PartitionSpec as P

AXES = ("ylo", "x", "yhi", "z", "core")
HSIZE = 128
HPG = 3
GROUPS = 16
BLOCK = 512
STATS = 16
FACTOR = 1.4426950408889634 / HSIZE**0.5
SCALE = 1.6
BF = jnp.bfloat16
F32 = jnp.float32
ANY = pl.BlockSpec(memory_space=pl.ANY)


def params(mib):
    return pltpu.CompilerParams(vmem_limit_bytes=mib * 2**20)


def cost(us):
    return pl.CostEstimate(flops=int(us * SCALE * 1.15e9), bytes_accessed=10**5, transcendentals=0)


def gate(a, *tokens):
    return pl.pallas_call(
        lambda *refs: None,
        in_specs=[ANY] * (1 + len(tokens)),
        out_specs=ANY,
        out_shape=jax.ShapeDtypeStruct(a.shape, a.dtype),
        input_output_aliases={0: 0},
        cost_estimate=cost(0.01),
    )(a, *tokens)


def group_of(dest):
    ylo, yhi, z = dest // 8, (dest // 4) % 2, dest % 4
    return yhi * 8 + z * 2 + ylo


def dequant_kernel(q_ref, k_ref, v_ref, qs_ref, ks_ref, vs_ref, *refs, heads):
    o_ref = refs[-1]
    scales = [r[...].astype(F32).T for r in (qs_ref, ks_ref, vs_ref)]
    scales[0] = scales[0] * FACTOR
    for dest in range(GROUPS):
        for i, head in enumerate(heads):
            col = group_of(dest) * HPG + head
            for part, ref in enumerate((q_ref, k_ref, v_ref)):
                at = i if part == 0 else len(heads) + 2 * i + part - 1
                vals = ref[:, col * HSIZE : (col + 1) * HSIZE].astype(F32)
                o_ref[dest, :, at * HSIZE : (at + 1) * HSIZE] = (
                    vals * scales[part][:, col : col + 1]
                ).astype(BF)


def dequant(heads, args, *tokens):
    tok = args[0].shape[0]
    return pl.pallas_call(
        functools.partial(dequant_kernel, heads=heads),
        in_specs=[pl.BlockSpec(memory_space=pltpu.VMEM)] * len(args) + [ANY] * len(tokens),
        out_shape=jax.ShapeDtypeStruct((GROUPS, tok, 3 * len(heads) * HSIZE), BF),
        compiler_params=params(56),
        cost_estimate=cost(3),
    )(*args, *tokens)


def attend_kernel(at_ref, *refs, pieces, queries, tokens):
    q_refs, refs = refs[:queries], refs[queries:]
    kv, refs = refs[: len(pieces)], refs[len(pieces) + tokens :]
    o_refs, vaug = refs[:-1], refs[-1]
    step = pl.program_id(0)

    @pl.when(step == 0)
    def _():
        vaug[:, HSIZE:] = jnp.ones((vaug.shape[0], HSIZE), BF)
        low = 0
        for ref, size in zip(kv, pieces):
            vaug[low : low + size, :HSIZE] = ref[:, HSIZE:]
            low += size

    query = q_refs[0][...]
    if queries > 1:
        query = jnp.where(step < 2, query, q_refs[1][...])

    def score(j):
        return lax.dot_general(
            query, kv[j][:, :HSIZE], (((1,), (1,)), ((), ())), preferred_element_type=F32
        )

    peak = accum = None
    now = score(0)
    low = 0
    for j, size in enumerate(pieces):
        later = score(j + 1) if j + 1 < len(pieces) else None
        top = jnp.max(now, axis=1, keepdims=True)
        newpeak = top if peak is None else jnp.maximum(peak, top)
        weight = jnp.exp2((now - newpeak).astype(BF))
        term = jnp.dot(weight, vaug[low : low + size, :], preferred_element_type=F32)
        accum = term if accum is None else accum * jnp.exp2(peak - newpeak) + term
        peak, now, low = newpeak, later, low + size
    total = accum[:, HSIZE:]
    out = (accum[:, :HSIZE] / total).astype(BF)
    logsum = peak + jnp.log2(total)
    line = logsum.T[:1, :]
    line = jnp.concatenate(
        [line[:, r * HSIZE : (r + 1) * HSIZE] for r in range(BLOCK // HSIZE)], axis=0
    )
    first = line.astype(BF).astype(F32)
    second = (line - first).astype(BF).astype(F32)
    third = line - first - second
    rows = jnp.concatenate([first, second, third, jnp.zeros_like(line)], axis=0).astype(BF)
    for i, o_ref in enumerate(o_refs):

        @pl.when(step // 2 == i)
        def _():
            o_ref[0, :BLOCK, :] = out
            o_ref[0, BLOCK:, :] = rows


def attend(ylo, queries, kv, tokens=()):
    n = len(queries)
    pieces = tuple(a.shape[0] for a, _ in kv)

    def query(i, col):
        return pl.BlockSpec(
            (BLOCK, HSIZE), lambda g, s: (((g if n == 1 else jnp.clip(g - 2 * i, 0, 1)) + s[0]) % 2, col)
        )

    def piece(a, col):
        return pl.BlockSpec((a.shape[0], 2 * HSIZE), lambda g, s: (0, col))

    def result(i):
        return pl.BlockSpec(
            (1, BLOCK + STATS, HSIZE), lambda g, s: (jnp.clip(g - 2 * i, 0, 1), 0, 0)
        )

    return pl.pallas_call(
        functools.partial(attend_kernel, pieces=pieces, queries=n, tokens=len(tokens)),
        grid_spec=pltpu.PrefetchScalarGridSpec(
            num_scalar_prefetch=1,
            grid=(2 * n,),
            in_specs=[
                *[query(i, col) for i, (_, col) in enumerate(queries)],
                *[piece(*a) for a in kv],
                *[ANY] * len(tokens),
            ],
            out_specs=[result(i) for i in range(n)],
            scratch_shapes=[pltpu.VMEM((sum(pieces), 2 * HSIZE), BF)],
        ),
        out_shape=[jax.ShapeDtypeStruct((2, BLOCK + STATS, HSIZE), BF)] * n,
        compiler_params=params(30),
        cost_estimate=cost(6.5 * n),
    )(ylo, *[a for a, _ in queries], *[a for a, _ in kv], *tokens)


def combine_kernel(a, b, *refs):
    outs = refs[-2:]

    def logsum(ref, half):
        s = ref[half, BLOCK:, :].astype(F32)
        s = s[:4] + s[4:8] + s[8:12]
        return jnp.concatenate(
            [jnp.broadcast_to(s[r : r + 1], (HSIZE, HSIZE)).T for r in range(4)], axis=0
        )

    for half in range(2):
        la, lb = logsum(a, half), logsum(b, half)
        top = jnp.maximum(la, lb)
        wa, wb = jnp.exp2(la - top), jnp.exp2(lb - top)
        out = a[half, :BLOCK, :].astype(F32) * wa + b[half, :BLOCK, :].astype(F32) * wb
        outs[half][...] = (out / (wa + wb)).astype(BF)


def combine(a, b, *tokens):
    vmem = pl.BlockSpec(memory_space=pltpu.VMEM)
    return pl.pallas_call(
        combine_kernel,
        in_specs=[vmem] * 2 + [ANY] * len(tokens),
        out_shape=[jax.ShapeDtypeStruct((BLOCK, HSIZE), BF)] * 2,
        compiler_params=params(12),
        cost_estimate=cost(2),
    )(a, b, *tokens)


def ring(n, step):
    return [(i, (i + step) % n) for i in range(n)]


def opposite_y(a, flip=False):
    perm = []
    for yhi in range(2):
        for core in range(2):
            perm.append((yhi * 2 + core, (1 - yhi) * 2 + (1 - core if flip else core)))
    return lax.ppermute(a, ("yhi", "core"), perm)


def swap(a):
    return lax.ppermute(a, "core", [(0, 1), (1, 0)])


def other_ylo(a):
    return lax.ppermute(a, "ylo", [(0, 1), (1, 0)])


def key_pair(a):
    return lax.ppermute(a, "x", [(0, 1), (1, 0), (2, 3), (3, 2)])


def query_pair(a):
    return lax.ppermute(a, "x", [(0, 3), (3, 0), (1, 2), (2, 1)])


def ring_gather(to_next, to_last, to_far):
    return [
        lax.ppermute(to_next, "z", ring(4, 1)),
        lax.ppermute(to_last, "z", ring(4, -1)),
        lax.ppermute(to_far, "z", ring(4, 2)),
    ]


def pack_kernel(w_ref, token_ref, o_ref):
    half = w_ref.shape[1] // 2
    width = half // 4
    for to in range(4):
        for yhi in range(2):
            low = yhi * half + to * width
            o_ref[to, :, yhi * width : (yhi + 1) * width] = w_ref[:, low : low + width]


def pack_weight(out_weight, token):
    rows, width = out_weight.shape
    return pl.pallas_call(
        pack_kernel,
        in_specs=[pl.BlockSpec(memory_space=pltpu.VMEM), ANY],
        out_shape=jax.ShapeDtypeStruct((4, rows, width // 4), BF),
        compiler_params=params(56),
        cost_estimate=cost(4),
    )(out_weight, token)


def project_kernel(at_ref, *refs, head, before, last, tokens):
    blocks, w, refs = refs[:4], refs[4:6], refs[6:]
    start, refs = refs[:before], refs[before + tokens :]
    outs, (left, right, sems) = refs[: 4 if last else 1], refs[4 if last else 1 :]
    cols = right.shape[1] // 4
    core, apart, yhi, z = at_ref[0], at_ref[1], at_ref[2], at_ref[3]
    copies = []
    for i, off in enumerate((0, 3, 1, 2) * 2):
        group = w[i // 4].at[lax.rem(z + off, 4)]
        for j in range(4):
            low = (lax.rem(yhi + 1 + j // 2, 2) * 2 + lax.rem(core + j, 2)) * cols
            copies.append(
                pltpu.make_async_copy(
                    group.at[pl.ds(head * HSIZE, HSIZE), pl.ds(pl.multiple_of(low, cols), cols)],
                    right.at[pl.ds(i * HSIZE, HSIZE), pl.ds(j * cols, cols)],
                    sems.at[len(copies)],
                )
            )
    for copy in copies:
        copy.start()
    for p in range(2):
        low = pl.multiple_of(lax.rem(apart + p, 2) * HSIZE, HSIZE)
        for r in range(4):
            at = (p * 4 + r) * HSIZE
            left[:, at : at + HSIZE] = blocks[r][:, pl.ds(low, HSIZE)]
    for copy in copies:
        copy.wait()
    out = jnp.dot(left[...], right[...], preferred_element_type=F32)
    if before:
        out = out + start[0][...]
    if last:
        for j in range(4):
            outs[j][...] = out[:, j * cols : (j + 1) * cols].astype(BF)
    else:
        outs[0][...] = out


def project(at, head, blocks, weights, before=(), last=False, tokens=()):
    cols = weights[0].shape[1]
    vmem = pl.BlockSpec(memory_space=pltpu.VMEM)
    if last:
        out_shape = [jax.ShapeDtypeStruct((BLOCK, cols), BF)] * 4
    else:
        out_shape = jax.ShapeDtypeStruct((BLOCK, 4 * cols), F32)
    return pl.pallas_call(
        functools.partial(
            project_kernel, head=head, before=len(before), last=last, tokens=len(tokens)
        ),
        in_specs=[pl.BlockSpec(memory_space=pltpu.SMEM)]
        + [vmem] * 4
        + [ANY] * 2
        + [vmem] * len(before)
        + [ANY] * len(tokens),
        out_shape=out_shape,
        scratch_shapes=[
            pltpu.VMEM((BLOCK, 8 * HSIZE), BF),
            pltpu.VMEM((8 * HSIZE, 4 * cols), BF),
            pltpu.SemaphoreType.DMA((32,)),
        ],
        compiler_params=params(20),
        cost_estimate=cost(3),
    )(at, *blocks, *weights, *before, *tokens)


def finish_kernel(core_ref, a, b, c, d, o_ref):
    own = (a[...].astype(F32) + b[...].astype(F32)).astype(BF)
    other = (c[...].astype(F32) + d[...].astype(F32)).astype(BF)
    tok = o_ref.shape[2]
    for i in range(o_ref.shape[0]):
        rows = slice(i * tok, (i + 1) * tok)
        o_ref[i, core_ref[0]] = own[rows]
        o_ref[i, 1 - core_ref[0]] = other[rows]


def finish(core, tok, *terms):
    rows, cols = terms[0].shape
    vmem = pl.BlockSpec(memory_space=pltpu.VMEM)
    return pl.pallas_call(
        finish_kernel,
        in_specs=[pl.BlockSpec(memory_space=pltpu.SMEM)] + [vmem] * 4,
        out_shape=jax.ShapeDtypeStruct((rows // tok, 2, tok, cols), BF),
        compiler_params=params(12),
        cost_estimate=cost(1),
    )(core, *terms).reshape(2 * rows, cols)


def on_device(q_vals, k_vals, v_vals, q_scale, k_scale, v_scale, out_weight):
    tok = q_vals.shape[0]
    ylo, yhi, z, core = (lax.axis_index(n) for n in ("ylo", "yhi", "z", "core"))
    mine = ylo.reshape(1)
    every = ("ylo", "yhi", "z")

    def exchange(a):
        a = lax.all_to_all(a, every, split_axis=0, concat_axis=0, tiled=True)
        return a.reshape(-1, a.shape[2])

    parts = (q_vals, k_vals, v_vals, q_scale.T, k_scale.T, v_scale.T)
    d1 = dequant((0, 1), parts)
    d2 = dequant((2,), parts, d1)
    packed = pack_weight(out_weight, d1)
    e1 = gate(exchange(d1), d2, packed)
    q1, kv0, kv1 = (e1[:, i * 2 * HSIZE : (i + 1) * 2 * HSIZE] for i in range(3))
    near0 = key_pair(kv0)
    theirs1 = query_pair(q1)
    s1 = swap(e1)
    e2 = exchange(gate(d2, e1))
    near1 = key_pair(gate(kv1, near0))
    snear0 = swap(near0)
    q2, kv2 = e2[:, :HSIZE], e2[:, HSIZE:]
    theirs2 = query_pair(q2)
    near2 = key_pair(gate(kv2, near1))
    s2 = swap(kv2)
    snear1, snear2 = swap(near1), swap(near2)
    moved = lax.all_to_all(gate(packed, e2), "z", split_axis=0, concat_axis=0, tiled=True)

    keys0 = [(e1, 1), (s1, 1), (near0, 0), (snear0, 0)]
    keys1 = [(e1, 2), (s1, 2), (near1, 0), (snear1, 0)]
    keys2 = [(kv2, 0), (s2, 0), (near2, 0), (snear2, 0)]

    def widen(keep, send):
        return jnp.concatenate([keep, other_ylo(send)], axis=1)

    def gather(both):
        return [both, *ring_gather(both, both, both)]

    (kept0,) = attend(mine, [(e1, 0)], keys0)
    (sent0,) = attend(mine, [(theirs1, 0)], keys0, (kept0,))
    back0 = query_pair(sent0)
    (sent1,) = attend(mine, [(theirs1, 1)], keys1, (sent0,))
    back1 = query_pair(sent1)
    rows0 = combine(kept0, back0, sent1)
    (kept1,) = attend(mine, [(e1, 1)], keys1, (rows0[0],))
    both0 = widen(*rows0)
    rows1 = combine(kept1, back1)
    (sent2,) = attend(mine, [(theirs2, 0)], keys2, (rows1[0], both0))
    set0 = gather(both0)
    back2 = query_pair(sent2)
    both1 = widen(*rows1)
    (kept2,) = attend(mine, [(q2, 0)], keys2, (sent2, both1))
    set1 = gather(both1)
    rows2 = combine(kept2, back2, *set0[1:])
    moved = gate(moved, rows2[0])
    weights = [moved, swap(moved)]
    both2 = widen(*rows2)
    set2 = gather(both2)
    at = jnp.stack([core, jnp.where(core == ylo, 0, 1), yhi, z])
    out = project(at, 0, set0, weights, tokens=(both2, *set1[1:]))
    out = project(at, 1, set1, weights, (out,))
    out = project(at, 2, set2, weights, (out,), last=True)
    return finish(
        core.reshape(1), tok, out[2], opposite_y(out[0]), swap(out[3]), opposite_y(out[1], flip=True)
    )


def solution(mesh):
    fine = Mesh(mesh.devices.reshape(2, 4, 2, 4, 2), AXES)
    return jax.shard_map(
        on_device,
        mesh=fine,
        in_specs=(P(AXES, None),) * 6 + (P(("yhi", "z", "core"), None),),
        out_specs=P(("ylo", "x"), ("yhi", "z", "core")),
        check_vma=False,
    )
```
